512 devices in a mesh: trade: 32 (over x, y), path: 16 (over z, core).
Axes of the slice: x: 4, y: 8, z: 8, core: 2. Of those that a mesh axis runs over, the one named last changes fastest.
Arguments:
- coef: bfloat16 [2, 64, 16384], P(None, None, 'trade'), may hold values from -0.75 to 0.75
- membership: int32 [16384], P('trade'), may hold values from 0 to 4095
- trade_type: int32 [16384], P('trade'), may hold values from 0 to 7
- type_notional: float32 [8], replicated, may hold values from 0.5 to 4
- basis_start: bfloat16 [64, 1024], P(None, 'path'), may hold values from -6 to 6
- shocks: bfloat16 [64, 1024], P(None, 'path'), may hold values from -6 to 6
- basis_map: bfloat16 [64, 64], replicated, may hold values from -0.75 to 0.75
- credit_weight: bfloat16 [2, 1024, 4096], P(None, 'path'), may hold values from 0.5 to 8
Outputs:
- exposure: float32 [2, 4096], P(None, 'trade')
- coef_grad: float32 [2, 64, 16384], P(None, None, 'trade')
- basis_grad: float32 [64, 1024], P(None, 'path')
The draws below stay inside these ranges and needn't reach their ends.
All inputs are finite; a program needn't handle non-finite values.
Results may differ from the reference program's by a relative error of at most 0.0029.
Values may be sent and summed in bfloat16 or wider, within the bound.
A program may use at most 64 MiB of HBM per device.

```python
import math
import jax
import jax.numpy as jnp
import numpy as np
from jax import lax

NB = 64
SETS = 4096
TYPES = 8
TRADES = 16384
PATHS = 1024


def set_ends(values, stream_key, least, largest):
    longest = values.shape.index(max(values.shape))
    spots = []
    for shift in (0, 1):
        where = [jax.random.randint(jax.random.fold_in(stream_key, axis), (), 0, length) for axis, length in enumerate(values.shape)]
        where[longest] = (where[longest] + shift) % values.shape[longest]
        spots.append(tuple(where))
    return values.at[spots[0]].set(least).at[spots[1]].set(largest)


def levels(stream_key, dims, shards, least, top_value):
    def one(position, blocks):
        heights = jax.random.uniform(jax.random.fold_in(jax.random.fold_in(stream_key, 6), position), (blocks,), jnp.float32, least / len(shards), top_value / len(shards))
        return jnp.repeat(jnp.exp(heights), dims[position] // blocks).reshape((-1,) + (1,) * (len(dims) - position - 1))

    factor_of = one(*shards[0])
    for cut in shards[1:]:
        factor_of = factor_of * one(*cut)
    return factor_of


def cumulative_ranks(amount, skew):
    loads = [(1 << 20) // math.isqrt(rank ** skew) + 1 for rank in range(1, amount + 1)]
    spread = 1 + sum(loads) // (1 << 30)
    return np.cumsum(np.array([max(1, weight // spread) for weight in loads]))


def ranked(key, shape, amount, skew):
    listing = cumulative_ranks(amount, skew)
    pick = jax.random.randint(jax.random.fold_in(key, 1), shape, 0, int(listing[amount - 1]))
    standing = jnp.searchsorted(jnp.asarray(listing, jnp.int32), pick, side="right")
    return jax.random.permutation(jax.random.fold_in(key, 2), amount)[standing].astype(jnp.int32)


def bell_draw(rng, shape, deviation, reach, split=(), kind=jnp.bfloat16):
    gain = levels(rng, shape, split, -0.22, 0.18) if split else 1.0
    values = jax.random.normal(rng, shape, jnp.float32) * deviation * gain
    return jnp.minimum(jnp.maximum(values, -reach), reach).astype(kind)


def setup_inputs(seed: int = 0) -> dict:
    seeds = jax.random.split(jax.random.key(seed), 9)
    coef = bell_draw(seeds[0], (2, NB, TRADES), NB ** -0.5, 0.75, ((2, 32),))
    membership = set_ends(ranked(seeds[1], (TRADES,), SETS, 1), jax.random.fold_in(seeds[1], 3), 0, SETS - 1).astype(jnp.int32)
    trade_type = set_ends(jax.random.randint(seeds[2], (TRADES,), 0, TYPES), jax.random.fold_in(seeds[2], 1), 0, TYPES - 1).astype(jnp.int32)
    type_notional = jnp.clip(jnp.exp(jax.random.uniform(seeds[3], (TYPES,), jnp.float32, math.log(0.5), math.log(4.0))), 0.5, 4.0)
    basis_start = bell_draw(seeds[4], (NB, PATHS), 1.0, 6.0, ((1, 16),))
    shocks = bell_draw(seeds[5], (NB, PATHS), 1.0, 6.0, ((1, 16),))
    basis_map = bell_draw(seeds[6], (NB, NB), NB ** -0.5, 0.75)
    credit_weight = jnp.clip(jnp.exp(math.log(8.0) - 2.7725887 * jax.random.uniform(seeds[7], (2, PATHS, SETS), jnp.float32) ** levels(seeds[7], (2, PATHS, SETS), ((1, 16),), -0.2, 0.2)), 0.5, 8.0).astype(jnp.bfloat16)
    return dict(coef=coef, membership=membership, trade_type=trade_type, type_notional=type_notional, basis_start=basis_start, shocks=shocks, basis_map=basis_map, credit_weight=credit_weight)


def reference(coef, membership, trade_type, type_notional, basis_start, shocks, basis_map, credit_weight):
    notional = type_notional[trade_type]
    pre = jnp.dot(basis_map.T, basis_start, preferred_element_type=jnp.float32)
    later = jnp.tanh(pre + shocks.astype(jnp.float32)).astype(jnp.bfloat16)
    bases = (basis_start, later)
    exposures = []
    grads = []
    pulls = []
    for step in range(2):
        values = (jnp.dot(bases[step].T, coef[step], preferred_element_type=jnp.float32) * notional[None, :]).astype(jnp.bfloat16)
        netted = jax.ops.segment_sum(values.astype(jnp.float32).T, membership, num_segments=SETS).T
        exposures.append(lax.optimization_barrier(jnp.mean(jax.nn.softplus(netted), axis=0)))
        set_adj = (credit_weight[step].astype(jnp.float32) * jax.nn.sigmoid(netted)).astype(jnp.bfloat16)
        trade_adj = (set_adj.astype(jnp.float32)[:, membership] * notional[None, :]).astype(jnp.bfloat16)
        grads.append(jnp.dot(bases[step], trade_adj, preferred_element_type=jnp.float32) / math.sqrt(PATHS))
        pulls.append(jnp.dot(coef[step], trade_adj.T, preferred_element_type=jnp.float32))
    slope = 1.0 - later.astype(jnp.float32) ** 2
    carried = jnp.dot(basis_map.astype(jnp.float32), pulls[1] * slope, precision=lax.Precision.HIGHEST)
    basis_grad = (pulls[0] + carried) / math.sqrt(TRADES)
    return (jnp.stack(exposures), jnp.stack(grads), basis_grad)
```

```python
import functools
import math

import jax
import jax.numpy as jnp
from jax import lax
from jax.experimental import pallas as pl
from jax.experimental.pallas import tpu as pltpu
from jax.sharding import PartitionSpec as P

MESH = pl.DeviceIdType.MESH
NT = 32
NY = 8
NP = 16
F32 = jnp.float32
BF16 = jnp.bfloat16


def dot(a, b):
    return jnp.dot(a, b, preferred_element_type=F32)


def dot_nt(a, b):
    return lax.dot_general(a, b, (((1,), (1,)), ((), ())), preferred_element_type=F32)


def split(v):
    high = v.astype(BF16)
    return high, (v - high.astype(F32)).astype(BF16)


def eye(rows, cols, shift):
    r = lax.broadcasted_iota(jnp.int32, (rows, cols), 0)
    c = lax.broadcasted_iota(jnp.int32, (rows, cols), 1)
    return (r + shift == c).astype(BF16)


def outward(step, count):
    half = lax.div(step + 1, 2)
    sign = 1 - 2 * lax.rem(step, 2)
    return lax.rem(count // 2 + half * sign + count, count)


def kernel(
    coef_in, member_in, kind_in, worth_in, start_in, shocks_in, bmap_in, cw,
    exp_out, coef_out, basis_out,
    coef, member, kind, worth, start, shocks, bmap, onehot, tsend, trecv, pk, bbuf, cwown, cwbuf, cown, fsend, call, net, gsend, gbuf,
    exsend, exbuf, qsend, qbuf, csend, cbuf, ssem, rsem, lsem,
):
    me_t = lax.axis_index("trade")
    me_p = lax.axis_index("path")
    x, y = lax.div(me_t, NY), lax.rem(me_t, NY)
    z, core = lax.div(me_p, 2), lax.rem(me_p, 2)
    date = lax.div(me_p, NP // 2)

    def trade_peer(step):
        dy = outward(lax.div(step, NT // NY), NY)
        dx = outward(lax.rem(step, NT // NY), NT // NY)
        return lax.rem(x + dx, NT // NY) * NY + lax.rem(y + dy, NY)

    def path_peer(step):
        dz = outward(lax.div(step, 2), NP // 2)
        dc = 1 - lax.rem(step, 2)
        return lax.rem(z + dz, NP // 2) * 2 + lax.rem(core + dc, 2)

    def put(src, dst, slot, dev):
        pltpu.make_async_remote_copy(
            src_ref=src, dst_ref=dst, send_sem=ssem.at[slot], recv_sem=rsem.at[slot],
            device_id=dev, device_id_type=MESH,
        ).start()

    def over_trade(src_of, dst, slot):
        def one(step, carry):
            peer = trade_peer(step)
            put(src_of(peer), dst.at[me_t], slot, (peer, me_p))
            return carry

        lax.fori_loop(0, NT - 1, one, 0)

    def over_path(src_of, dst, slot):
        def one(step, carry):
            peer = path_peer(step)
            put(src_of(peer), dst.at[me_p], slot, (me_t, peer))
            return carry

        lax.fori_loop(0, NP - 1, one, 0)

    def arrived(ref, slot):
        pltpu.make_async_copy(ref, ref, rsem.at[slot]).wait()

    def sent(ref, slot):
        pltpu.make_async_copy(ref, ref, ssem.at[slot]).wait()

    barrier = pltpu.get_barrier_semaphore()

    def greet_trade(step, carry):
        pl.semaphore_signal(barrier, inc=1, device_id=(trade_peer(step), me_p), device_id_type=MESH)
        return carry

    def greet_path(step, carry):
        pl.semaphore_signal(barrier, inc=1, device_id=(me_t, path_peer(step)), device_id_type=MESH)
        return carry

    lax.fori_loop(0, NT - 1, greet_trade, 0)
    lax.fori_loop(0, NP - 1, greet_path, 0)

    sets = pl.ds(pl.multiple_of(me_t * 128, 128), 128)
    loads = [
        pltpu.make_async_copy(src, dst, lsem.at[n])
        for n, (src, dst) in enumerate((
            (start_in, start), (shocks_in, shocks), (bmap_in, bmap), (kind_in, kind),
            (worth_in, worth), (member_in, member), (coef_in.at[2 * date + core], coef),
            (cw.at[:, :, sets], cwown),
        ))
    ]
    for load in loads:
        load.start()
    for load in loads[:-1]:
        load.wait()

    kinds = kind[...]
    notional = jnp.zeros(kinds.shape, F32)
    for n in range(8):
        notional = jnp.where(kinds == n, worth[0:1, n : n + 1], notional)
    eye64 = eye(64, 64, 0)
    left, right = eye(64, 128, 0), eye(64, 128, 64)
    start_t = dot_nt(eye64, start[...]).astype(BF16)
    later_t = jnp.tanh(dot(start_t, bmap[...]) + dot_nt(eye64, shocks[...])).astype(BF16)
    slope = 1.0 - dot_nt(eye64, later_t) ** 2
    bases = (start_t, later_t)

    def pack(v):
        return (dot(v[0:32], left) + dot(v[32:64], right)).astype(BF16)

    pk[0] = pack(start_t)
    pk[1] = pack(later_t)

    high, low = split(coef[...].astype(F32) * notional)
    both = jnp.concatenate([high, low], axis=0)
    members = member[...]

    def by_set(b, carry):
        ids = lax.broadcasted_iota(jnp.int32, (128, 512), 0) + b * 128
        hot = (members == ids).astype(F32).astype(BF16)
        onehot[b] = hot
        part = dot_nt(both, hot)
        tsend[b] = (part[0:32] + part[32:64]).astype(BF16)
        return carry

    lax.fori_loop(0, NT, by_set, 0, unroll=2)
    trecv[me_t] = tsend[me_t]

    pl.semaphore_wait(barrier, NT + NP - 2)
    over_trade(lambda peer: tsend.at[peer], trecv, 0)
    over_path(lambda peer: pk.at[lax.div(peer, NP // 2)], bbuf, 1)
    over_path(lambda peer: cw.at[lax.div(peer, NP // 2), :, sets], cwbuf, 2)
    loads[-1].wait()
    bbuf[me_p] = pk[date]
    cwbuf[me_p] = cwown[date]

    arrived(trecv.at[pl.ds(0, NT - 1)], 0)
    total = trecv[0].astype(F32)
    for n in range(1, NT):
        total = total + trecv[n].astype(F32)
    mine = 2 * date + core
    cown[core] = total
    fsend[...] = total.astype(BF16)
    far = lax.rem(z + NP // 4, NP // 2)
    put(cown.at[core], cown.at[core], 3, (me_t, 2 * z + 1 - core))
    put(fsend, call.at[mine], 4, (me_t, 2 * far + core))
    put(fsend, call.at[mine], 4, (me_t, 2 * far + 1 - core))

    arrived(bbuf.at[pl.ds(0, NP - 1)], 1)
    arrived(cwbuf.at[pl.ds(0, NP - 1)], 2)
    packed = bbuf[...].reshape(512, 128)
    q = lax.rem(me_p, NP // 2)
    r = lax.broadcasted_iota(jnp.int32, (16, 128), 0)
    c = lax.broadcasted_iota(jnp.int32, (16, 128), 1)
    want = jnp.where(r < 8, 8 * q + r, 56 + 8 * q + r)
    rows_b = dot_nt((c == want).astype(F32).astype(BF16), packed).astype(BF16)

    arrived(cown.at[0], 3)
    none = jnp.zeros((64, 128), BF16)
    weights = []
    for part in split(cown[...].reshape(64, 128)):
        weights.append(jnp.concatenate([part, none], axis=1))
        weights.append(jnp.concatenate([none, part], axis=1))
    call[pl.ds(2 * date, 2)] = cown[...].astype(BF16)
    netted = dot(jnp.concatenate([packed, packed], axis=1), jnp.concatenate(weights, axis=0))
    net[...] = netted
    cw_a = cwbuf[:, 0:32, :].reshape(512, 128).astype(F32)
    cw_b = cwbuf[:, 32:64, :].reshape(512, 128).astype(F32)
    adj_a = (cw_a * jax.nn.sigmoid(netted[:, 0:128])).astype(BF16)
    adj_b = (cw_b * jax.nn.sigmoid(netted[:, 128:256])).astype(BF16)
    grad = dot(rows_b[0:8], adj_a) + dot(rows_b[8:16], adj_b)
    gsend[...] = grad
    gbuf[me_t] = grad
    over_trade(lambda peer: gsend, gbuf, 5)

    wide = net[...]
    soft = jnp.maximum(wide, 0.0) + jnp.log1p(jnp.exp(-jnp.abs(wide)))
    soft = jnp.sum(soft, axis=0, keepdims=True)
    exposure = (soft[:, 0:128] + soft[:, 128:256]) / 1024.0
    exsend[...] = jnp.broadcast_to(exposure, (8, 128))
    put(exsend, exbuf, 6, (me_t, lax.rem(me_p + NP // 2, NP)))

    arrived(call.at[pl.ds(0, 2)], 4)
    pulls = []
    for t in range(2):
        c_t = call[2 * t : 2 * t + 2].reshape(64, 128)
        adj = (cwown[t].astype(F32) * jax.nn.sigmoid(dot(bases[t], c_t))).astype(BF16)
        pulls.append(dot_nt(c_t, adj))
    high, low = split(pulls[1] * slope)
    carried = dot(bmap[...], high) + dot(bmap[...], low)
    partial = pack(((pulls[0] + carried) / 128.0).astype(BF16))
    qsend[...] = partial
    qbuf[me_t] = partial
    over_trade(lambda peer: qsend, qbuf, 7)

    arrived(gbuf.at[pl.ds(0, NT - 1)], 5)
    rows = jnp.zeros((16, 512), F32)
    for n in range(0, NT, 4):
        part = jnp.concatenate([gbuf[n + m] for m in range(4)], axis=1)
        high, low = split(part)
        rows = rows + dot(
            jnp.concatenate([high, low], axis=0), onehot[n : n + 4].reshape(512, 512)
        )
    rows = (rows[0:8] + rows[8:16]) * (notional / 32.0)
    folded = jnp.concatenate([rows[:, 0:256], rows[:, 256:512]], axis=0).astype(BF16)
    csend[...] = folded
    cbuf[me_p] = folded
    over_path(lambda peer: csend, cbuf, 8)

    arrived(qbuf.at[pl.ds(0, NT - 1)], 7)
    total = qbuf[0].astype(F32)
    for n in range(1, NT):
        total = total + qbuf[n].astype(F32)
    basis_out[0:32, :] = total[:, 0:64]
    basis_out[32:64, :] = pltpu.roll(total, 64, 1)[:, 0:64]

    arrived(exbuf, 6)
    row = lax.broadcasted_iota(jnp.int32, (2, 128), 0)
    exp_out[...] = jnp.where(row == date, exsend[0:2, :], exbuf[0:2, :])

    arrived(cbuf.at[pl.ds(0, NP - 1)], 8)
    for n in range(NP):
        t, k = n // 8, 8 * (n % 8)
        block = cbuf[n].astype(F32)
        coef_out[t, k : k + 8, 0:256] = block[0:8]
        coef_out[t, k : k + 8, 256:512] = block[8:16]

    sent(trecv.at[pl.ds(0, NT - 1)], 0)
    sent(bbuf.at[pl.ds(0, NP - 1)], 1)
    sent(cwbuf.at[pl.ds(0, NP - 1)], 2)
    sent(cown.at[0], 3)
    sent(call.at[pl.ds(0, 2)], 4)
    sent(gbuf.at[pl.ds(0, NT - 1)], 5)
    sent(exbuf, 6)
    sent(qbuf.at[pl.ds(0, NT - 1)], 7)
    sent(cbuf.at[pl.ds(0, NP - 1)], 8)


def shards(
    coef, membership, trade_type, type_notional, basis_start, shocks, basis_map, credit_weight
):
    vmem = pl.BlockSpec(memory_space=pltpu.VMEM)
    hbm = pl.BlockSpec(memory_space=pltpu.HBM)
    return pl.pallas_call(
        kernel,
        out_shape=(
            jax.ShapeDtypeStruct((2, 128), F32),
            jax.ShapeDtypeStruct((2, 64, 512), F32),
            jax.ShapeDtypeStruct((64, 64), F32),
        ),
        in_specs=[hbm] * 8,
        out_specs=(vmem, vmem, vmem),
        scratch_shapes=[
            pltpu.VMEM((32, 512), BF16),
            pltpu.VMEM((1, 512), jnp.int32),
            pltpu.VMEM((1, 512), jnp.int32),
            pltpu.VMEM((1, 8), F32),
            pltpu.VMEM((64, 64), BF16),
            pltpu.VMEM((64, 64), BF16),
            pltpu.VMEM((64, 64), BF16),
            pltpu.VMEM((NT, 128, 512), BF16),
            pltpu.VMEM((NT, 32, 128), BF16),
            pltpu.VMEM((NT, 32, 128), BF16),
            pltpu.VMEM((2, 32, 128), BF16),
            pltpu.VMEM((NP, 32, 128), BF16),
            pltpu.VMEM((2, 64, 128), BF16),
            pltpu.VMEM((NP, 64, 128), BF16),
            pltpu.VMEM((2, 32, 128), F32),
            pltpu.VMEM((32, 128), BF16),
            pltpu.VMEM((4, 32, 128), BF16),
            pltpu.VMEM((512, 256), F32),
            pltpu.VMEM((8, 128), F32),
            pltpu.VMEM((NT, 8, 128), F32),
            pltpu.VMEM((8, 128), F32),
            pltpu.VMEM((8, 128), F32),
            pltpu.VMEM((32, 128), BF16),
            pltpu.VMEM((NT, 32, 128), BF16),
            pltpu.VMEM((16, 256), BF16),
            pltpu.VMEM((NP, 16, 256), BF16),
            pltpu.SemaphoreType.DMA((9,)),
            pltpu.SemaphoreType.DMA((9,)),
            pltpu.SemaphoreType.DMA((8,)),
        ],
        compiler_params=pltpu.CompilerParams(
            collective_id=0, has_side_effects=True, vmem_limit_bytes=40 * 2**20
        ),
    )(*(pltpu.with_memory_space_constraint(v, pltpu.HBM) for v in (
        coef.reshape(4, 32, 512), membership.reshape(1, 512), trade_type.reshape(1, 512),
        type_notional.reshape(1, 8), basis_start, shocks, basis_map, credit_weight,
    )))


def solution(mesh):
    placed = (
        P(None, None, "trade"),
        P("trade"),
        P("trade"),
        P(),
        P(None, "path"),
        P(None, "path"),
        P(),
        P(None, "path", None),
    )
    return jax.shard_map(
        shards,
        mesh=mesh,
        in_specs=placed,
        out_specs=(P(None, "trade"), P(None, None, "trade"), P(None, "path")),
        check_vma=False,
    )
```

```python
import functools
import math

import jax
import jax.numpy as jnp
from jax import lax
from jax.experimental import pallas as pl
from jax.experimental.pallas import tpu as pltpu
from jax.sharding import PartitionSpec as P

MESH = pl.DeviceIdType.MESH
NT = 32
NY = 8
NP = 16
F32 = jnp.float32
BF16 = jnp.bfloat16


def dot(a, b):
    return jnp.dot(a, b, preferred_element_type=F32)


def dot_nt(a, b):
    return lax.dot_general(a, b, (((1,), (1,)), ((), ())), preferred_element_type=F32)


def split(v):
    high = v.astype(BF16)
    return high, (v - high.astype(F32)).astype(BF16)


def eye(rows, cols, shift):
    r = lax.broadcasted_iota(jnp.int32, (rows, cols), 0)
    c = lax.broadcasted_iota(jnp.int32, (rows, cols), 1)
    return (r + shift == c).astype(BF16)


def hops(offset, count):
    return min(offset, count - offset)


def farthest_first(offsets, counts):
    return sorted(offsets, key=lambda o: -sum(hops(v, n) for v, n in zip(o, counts)))


NX = NT // NY
NZ = NP // 2
TRADE_PEERS = farthest_first([(a, b) for a in range(NX) for b in range(NY)], (NX, NY))[:-1]
PATH_PEERS = farthest_first([(a, b) for a in range(NZ) for b in range(2)], (NZ, 2))[:-1]


def kernel(
    coef_in, member_in, kind_in, worth_in, start_in, shocks_in, bmap_in, cw,
    exp_out, coef_out, basis_out,
    coef, member, kind, worth, start, shocks, bmap, onehot, tsend, trecv, psend, pbuf, cown, fsend, call, net, gsend, gbuf,
    exsend, exbuf, qsend, qbuf, csend, cbuf, ssem, rsem, lsem,
):
    me_t = lax.axis_index("trade")
    me_p = lax.axis_index("path")
    x, y = lax.div(me_t, NY), lax.rem(me_t, NY)
    z, core = lax.div(me_p, 2), lax.rem(me_p, 2)
    date = lax.div(me_p, NP // 2)

    xs = [lax.rem(x + n, NX) * NY for n in range(NX)]
    ys = [lax.rem(y + n, NY) for n in range(NY)]
    zs = [lax.rem(z + n, NZ) for n in range(NZ)]
    cores = [core, 1 - core]
    trade_peers = [xs[a] + ys[b] for a, b in TRADE_PEERS]
    path_peers = [2 * zs[a] + cores[b] for a, b in PATH_PEERS]

    def put(src, dst, slot, dev):
        pltpu.make_async_remote_copy(
            src_ref=src, dst_ref=dst, send_sem=ssem.at[slot], recv_sem=rsem.at[slot],
            device_id=dev, device_id_type=MESH,
        ).start()

    def over_trade(src_of, dst, slot):
        for peer in trade_peers:
            put(src_of(peer), dst.at[me_t], slot, (peer, me_p))

    def over_path(src_of, dst, slot):
        for peer in path_peers:
            put(src_of(peer), dst.at[me_p], slot, (me_t, peer))

    def arrived(ref, slot):
        pltpu.make_async_copy(ref, ref, rsem.at[slot]).wait()

    def sent(ref, slot):
        pltpu.make_async_copy(ref, ref, ssem.at[slot]).wait()

    barrier = pltpu.get_barrier_semaphore()

    for peer in trade_peers:
        pl.semaphore_signal(barrier, inc=1, device_id=(peer, me_p), device_id_type=MESH)
    for peer in path_peers:
        pl.semaphore_signal(barrier, inc=1, device_id=(me_t, peer), device_id_type=MESH)

    sets = pl.ds(pl.multiple_of(me_t * 128, 128), 128)
    loads = [
        pltpu.make_async_copy(src, dst, lsem.at[n])
        for n, (src, dst) in enumerate((
            (start_in, start), (shocks_in, shocks), (bmap_in, bmap), (kind_in, kind),
            (worth_in, worth), (member_in, member), (coef_in.at[2 * date + core], coef),
            (cw.at[:, :, sets], psend.at[:, 0:64, :]),
        ))
    ]
    for load in loads:
        load.start()
    for load in loads:
        load.wait()

    kinds = kind[...]
    notional = jnp.zeros(kinds.shape, F32)
    for n in range(8):
        notional = jnp.where(kinds == n, worth[0:1, n : n + 1], notional)
    eye64 = eye(64, 64, 0)
    left, right = eye(64, 128, 0), eye(64, 128, 64)
    start_t = dot_nt(eye64, start[...]).astype(BF16)
    later_t = jnp.tanh(dot(start_t, bmap[...]) + dot_nt(eye64, shocks[...])).astype(BF16)
    slope = 1.0 - dot_nt(eye64, later_t) ** 2
    bases = (start_t, later_t)

    def pack(v):
        return (dot(v[0:32], left) + dot(v[32:64], right)).astype(BF16)

    psend[0, 64:96, :] = pack(start_t)
    psend[1, 64:96, :] = pack(later_t)
    pbuf[core, z] = psend[date]

    high, low = split(coef[...].astype(F32) * notional)
    both = jnp.concatenate([high, low], axis=0)
    members = member[...]

    def by_set(b, carry):
        ids = lax.broadcasted_iota(jnp.int32, (128, 512), 0) + b * 128
        hot = (members == ids).astype(F32).astype(BF16)
        onehot[b] = hot
        part = dot_nt(both, hot)
        tsend[b] = (part[0:32] + part[32:64]).astype(BF16)
        return carry

    lax.fori_loop(0, NT, by_set, 0, unroll=2)
    trecv[me_t] = tsend[me_t]

    pl.semaphore_wait(barrier, NT + NP - 2)
    for n in (4, 3, 5, 2, 6, 1, 7):
        put(psend.at[lax.div(zs[n], NZ // 2)], pbuf.at[core, z], 1, (me_t, 2 * zs[n] + core))
    over_trade(lambda peer: tsend.at[peer], trecv, 0)

    arrived(pbuf.at[0, pl.ds(0, NZ - 1)], 1)
    put(pbuf.at[core], pbuf.at[core], 2, (me_t, 2 * z + 1 - core))

    arrived(trecv.at[pl.ds(0, NT - 1)], 0)
    total = trecv[0].astype(F32)
    for n in range(1, NT):
        total = total + trecv[n].astype(F32)
    mine = 2 * date + core
    cown[core] = total
    fsend[...] = total.astype(BF16)
    far = zs[NZ // 2]
    put(cown.at[core], cown.at[core], 3, (me_t, 2 * z + 1 - core))
    put(fsend, call.at[mine], 4, (me_t, 2 * far + core))
    put(fsend, call.at[mine], 4, (me_t, 2 * far + 1 - core))

    arrived(pbuf.at[0], 2)
    packed = pbuf[:, :, 64:96, :].reshape(512, 128)
    q = lax.rem(me_p, NP // 2)
    r = lax.broadcasted_iota(jnp.int32, (16, 128), 0)
    c = lax.broadcasted_iota(jnp.int32, (16, 128), 1)
    want = jnp.where(r < 8, 8 * q + r, 56 + 8 * q + r)
    rows_b = dot_nt((c == want).astype(F32).astype(BF16), packed).astype(BF16)

    arrived(cown.at[0], 3)
    none = jnp.zeros((64, 128), BF16)
    weights = []
    for part in split(cown[...].reshape(64, 128)):
        weights.append(jnp.concatenate([part, none], axis=1))
        weights.append(jnp.concatenate([none, part], axis=1))
    call[pl.ds(2 * date, 2)] = cown[...].astype(BF16)
    netted = dot(jnp.concatenate([packed, packed], axis=1), jnp.concatenate(weights, axis=0))
    net[...] = netted
    cw_a = pbuf[:, :, 0:32, :].reshape(512, 128).astype(F32)
    cw_b = pbuf[:, :, 32:64, :].reshape(512, 128).astype(F32)
    adj_a = (cw_a * jax.nn.sigmoid(netted[:, 0:128])).astype(BF16)
    adj_b = (cw_b * jax.nn.sigmoid(netted[:, 128:256])).astype(BF16)
    grad = dot(rows_b[0:8], adj_a) + dot(rows_b[8:16], adj_b)
    gsend[...] = grad
    gbuf[me_t] = grad
    over_trade(lambda peer: gsend, gbuf, 5)

    wide = net[...]
    soft = jnp.maximum(wide, 0.0) + jnp.log1p(jnp.exp(-jnp.abs(wide)))
    soft = jnp.sum(soft, axis=0, keepdims=True)
    exposure = (soft[:, 0:128] + soft[:, 128:256]) / 1024.0
    exsend[...] = jnp.broadcast_to(exposure, (8, 128))
    put(exsend, exbuf, 6, (me_t, lax.rem(me_p + NP // 2, NP)))

    arrived(call.at[pl.ds(0, 2)], 4)
    pulls = []
    for t in range(2):
        c_t = call[2 * t : 2 * t + 2].reshape(64, 128)
        adj = (psend[t, 0:64, :].astype(F32) * jax.nn.sigmoid(dot(bases[t], c_t))).astype(BF16)
        pulls.append(dot_nt(c_t, adj))
    high, low = split(pulls[1] * slope)
    carried = dot(bmap[...], high) + dot(bmap[...], low)
    partial = pack(((pulls[0] + carried) / 128.0).astype(BF16))
    qsend[...] = partial
    qbuf[me_t] = partial
    over_trade(lambda peer: qsend, qbuf, 7)

    arrived(gbuf.at[pl.ds(0, NT - 1)], 5)
    rows = jnp.zeros((16, 512), F32)
    for n in range(0, NT, 4):
        part = jnp.concatenate([gbuf[n + m] for m in range(4)], axis=1)
        high, low = split(part)
        rows = rows + dot(
            jnp.concatenate([high, low], axis=0), onehot[n : n + 4].reshape(512, 512)
        )
    rows = (rows[0:8] + rows[8:16]) * (notional / 32.0)
    folded = jnp.concatenate([rows[:, 0:256], rows[:, 256:512]], axis=0).astype(BF16)
    csend[...] = folded
    cbuf[me_p] = folded
    over_path(lambda peer: csend, cbuf, 8)

    arrived(qbuf.at[pl.ds(0, NT - 1)], 7)
    total = qbuf[0].astype(F32)
    for n in range(1, NT):
        total = total + qbuf[n].astype(F32)
    basis_out[0:32, :] = total[:, 0:64]
    basis_out[32:64, :] = pltpu.roll(total, 64, 1)[:, 0:64]

    arrived(exbuf, 6)
    row = lax.broadcasted_iota(jnp.int32, (2, 128), 0)
    exp_out[...] = jnp.where(row == date, exsend[0:2, :], exbuf[0:2, :])

    arrived(cbuf.at[pl.ds(0, NP - 1)], 8)
    for n in range(NP):
        t, k = n // 8, 8 * (n % 8)
        block = cbuf[n].astype(F32)
        coef_out[t, k : k + 8, 0:256] = block[0:8]
        coef_out[t, k : k + 8, 256:512] = block[8:16]

    sent(trecv.at[pl.ds(0, NT - 1)], 0)
    sent(pbuf.at[0, pl.ds(0, NZ - 1)], 1)
    sent(pbuf.at[0], 2)
    sent(cown.at[0], 3)
    sent(call.at[pl.ds(0, 2)], 4)
    sent(gbuf.at[pl.ds(0, NT - 1)], 5)
    sent(exbuf, 6)
    sent(qbuf.at[pl.ds(0, NT - 1)], 7)
    sent(cbuf.at[pl.ds(0, NP - 1)], 8)


def shards(
    coef, membership, trade_type, type_notional, basis_start, shocks, basis_map, credit_weight
):
    vmem = pl.BlockSpec(memory_space=pltpu.VMEM)
    hbm = pl.BlockSpec(memory_space=pltpu.HBM)
    return pl.pallas_call(
        kernel,
        out_shape=(
            jax.ShapeDtypeStruct((2, 128), F32),
            jax.ShapeDtypeStruct((2, 64, 512), F32),
            jax.ShapeDtypeStruct((64, 64), F32),
        ),
        in_specs=[hbm] * 8,
        out_specs=(vmem, vmem, vmem),
        scratch_shapes=[
            pltpu.VMEM((32, 512), BF16),
            pltpu.VMEM((1, 512), jnp.int32),
            pltpu.VMEM((1, 512), jnp.int32),
            pltpu.VMEM((1, 8), F32),
            pltpu.VMEM((64, 64), BF16),
            pltpu.VMEM((64, 64), BF16),
            pltpu.VMEM((64, 64), BF16),
            pltpu.VMEM((NT, 128, 512), BF16),
            pltpu.VMEM((NT, 32, 128), BF16),
            pltpu.VMEM((NT, 32, 128), BF16),
            pltpu.VMEM((2, 96, 128), BF16),
            pltpu.VMEM((2, NP // 2, 96, 128), BF16),
            pltpu.VMEM((2, 32, 128), F32),
            pltpu.VMEM((32, 128), BF16),
            pltpu.VMEM((4, 32, 128), BF16),
            pltpu.VMEM((512, 256), F32),
            pltpu.VMEM((8, 128), F32),
            pltpu.VMEM((NT, 8, 128), F32),
            pltpu.VMEM((8, 128), F32),
            pltpu.VMEM((8, 128), F32),
            pltpu.VMEM((32, 128), BF16),
            pltpu.VMEM((NT, 32, 128), BF16),
            pltpu.VMEM((16, 256), BF16),
            pltpu.VMEM((NP, 16, 256), BF16),
            pltpu.SemaphoreType.DMA((9,)),
            pltpu.SemaphoreType.DMA((9,)),
            pltpu.SemaphoreType.DMA((8,)),
        ],
        compiler_params=pltpu.CompilerParams(
            collective_id=0, has_side_effects=True, vmem_limit_bytes=40 * 2**20
        ),
    )(*(pltpu.with_memory_space_constraint(v, pltpu.HBM) for v in (
        coef.reshape(4, 32, 512), membership.reshape(1, 512), trade_type.reshape(1, 512),
        type_notional.reshape(1, 8), basis_start, shocks, basis_map, credit_weight,
    )))


def solution(mesh):
    placed = (
        P(None, None, "trade"),
        P("trade"),
        P("trade"),
        P(),
        P(None, "path"),
        P(None, "path"),
        P(),
        P(None, "path", None),
    )
    return jax.shard_map(
        shards,
        mesh=mesh,
        in_specs=placed,
        out_specs=(P(None, "trade"), P(None, None, "trade"), P(None, "path")),
        check_vma=False,
    )
```

```python
import functools
import math

import jax
import jax.numpy as jnp
from jax import lax
from jax.experimental import pallas as pl
from jax.experimental.pallas import tpu as pltpu
from jax.sharding import PartitionSpec as P

MESH = pl.DeviceIdType.MESH
NT = 32
NY = 8
NP = 16
F32 = jnp.float32
BF16 = jnp.bfloat16


def dot(a, b):
    return jnp.dot(a, b, preferred_element_type=F32)


def dot_nt(a, b):
    return lax.dot_general(a, b, (((1,), (1,)), ((), ())), preferred_element_type=F32)


def split(v):
    high = v.astype(BF16)
    return high, (v - high.astype(F32)).astype(BF16)


def eye(rows, cols, shift):
    r = lax.broadcasted_iota(jnp.int32, (rows, cols), 0)
    c = lax.broadcasted_iota(jnp.int32, (rows, cols), 1)
    return (r + shift == c).astype(BF16)


def hops(offset, count):
    return min(offset, count - offset)


def farthest_first(offsets, counts):
    return sorted(offsets, key=lambda o: -sum(hops(v, n) for v, n in zip(o, counts)))


NX = NT // NY
NZ = NP // 2
TRADE_PEERS = farthest_first([(a, b) for a in range(NX) for b in range(NY)], (NX, NY))[:-1]
PATH_PEERS = farthest_first([(a, b) for a in range(NZ) for b in range(2)], (NZ, 2))[:-1]


def kernel(
    coef_in, member_in, kind_in, worth_in, start_in, shocks_in, bmap_in, cw,
    exp_out, coef_out, basis_out,
    coef, member, kind, worth, start, shocks, bmap, onehot, tsend, trecv, psend, pbuf, cown, fsend, call, net, gsend, gbuf,
    exsend, exbuf, qsend, qbuf, csend, cbuf, ssem, rsem, lsem,
):
    me_t = lax.axis_index("trade")
    me_p = lax.axis_index("path")
    x, y = lax.div(me_t, NY), lax.rem(me_t, NY)
    z, core = lax.div(me_p, 2), lax.rem(me_p, 2)
    date = lax.div(me_p, NP // 2)

    xs = [lax.rem(x + n, NX) * NY for n in range(NX)]
    ys = [lax.rem(y + n, NY) for n in range(NY)]
    zs = [lax.rem(z + n, NZ) for n in range(NZ)]
    cores = [core, 1 - core]
    trade_peers = [xs[a] + ys[b] for a, b in TRADE_PEERS]
    path_peers = [2 * zs[a] + cores[b] for a, b in PATH_PEERS]

    def put(src, dst, slot, dev):
        pltpu.make_async_remote_copy(
            src_ref=src, dst_ref=dst, send_sem=ssem.at[slot], recv_sem=rsem.at[slot],
            device_id=dev, device_id_type=MESH,
        ).start()

    def over_trade(src_of, dst, slot):
        for peer in trade_peers:
            put(src_of(peer), dst.at[me_t], slot, (peer, me_p))

    def over_path(src_of, dst, slot):
        for peer in path_peers:
            put(src_of(peer), dst.at[me_p], slot, (me_t, peer))

    def arrived(ref, slot):
        pltpu.make_async_copy(ref, ref, rsem.at[slot]).wait()

    def sent(ref, slot):
        pltpu.make_async_copy(ref, ref, ssem.at[slot]).wait()

    barrier = pltpu.get_barrier_semaphore()

    for peer in trade_peers:
        pl.semaphore_signal(barrier, inc=1, device_id=(peer, me_p), device_id_type=MESH)
    for peer in path_peers:
        pl.semaphore_signal(barrier, inc=1, device_id=(me_t, peer), device_id_type=MESH)

    sets = pl.ds(pl.multiple_of(me_t * 128, 128), 128)
    loads = [
        pltpu.make_async_copy(src, dst, lsem.at[n])
        for n, (src, dst) in enumerate((
            (start_in, start), (shocks_in, shocks), (bmap_in, bmap), (kind_in, kind),
            (worth_in, worth), (member_in, member), (coef_in.at[2 * date + core], coef),
            (cw.at[:, :, sets], psend.at[:, 0:64, :]),
        ))
    ]
    for load in loads:
        load.start()
    for load in loads[3:7]:
        load.wait()

    kinds = kind[...]
    notional = jnp.zeros(kinds.shape, F32)
    for n in range(8):
        notional = jnp.where(kinds == n, worth[0:1, n : n + 1], notional)
    high, low = split(coef[...].astype(F32) * notional)
    both = jnp.concatenate([high, low], axis=0)
    members = member[...]

    def by_set(b, carry):
        ids = lax.broadcasted_iota(jnp.int32, (128, 512), 0) + b * 128
        hot = (members == ids).astype(F32).astype(BF16)
        onehot[b] = hot
        part = dot_nt(both, hot)
        tsend[b] = (part[0:32] + part[32:64]).astype(BF16)
        return carry

    lax.fori_loop(0, NT, by_set, 0, unroll=2)
    trecv[me_t] = tsend[me_t]

    pl.semaphore_wait(barrier, NT + NP - 2)
    over_trade(lambda peer: tsend.at[peer], trecv, 0)

    for load in loads[:3] + loads[7:]:
        load.wait()
    eye64 = eye(64, 64, 0)
    left, right = eye(64, 128, 0), eye(64, 128, 64)
    start_t = dot_nt(eye64, start[...]).astype(BF16)
    later_t = jnp.tanh(dot(start_t, bmap[...]) + dot_nt(eye64, shocks[...])).astype(BF16)
    slope = 1.0 - dot_nt(eye64, later_t) ** 2
    bases = (start_t, later_t)

    def pack(v):
        return (dot(v[0:32], left) + dot(v[32:64], right)).astype(BF16)

    psend[0, 64:96, :] = pack(start_t)
    psend[1, 64:96, :] = pack(later_t)
    pbuf[core, z] = psend[date]

    for n in (4, 3, 5, 2, 6, 1, 7):
        put(psend.at[lax.div(zs[n], NZ // 2)], pbuf.at[core, z], 1, (me_t, 2 * zs[n] + core))

    arrived(pbuf.at[0, pl.ds(0, NZ - 1)], 1)
    put(pbuf.at[core], pbuf.at[core], 2, (me_t, 2 * z + 1 - core))

    arrived(trecv.at[pl.ds(0, NT - 1)], 0)
    total = trecv[0].astype(F32)
    for n in range(1, NT):
        total = total + trecv[n].astype(F32)
    mine = 2 * date + core
    cown[core] = total
    fsend[...] = total.astype(BF16)
    far = zs[NZ // 2]
    put(cown.at[core], cown.at[core], 3, (me_t, 2 * z + 1 - core))
    put(fsend, call.at[mine], 4, (me_t, 2 * far + core))
    put(fsend, call.at[mine], 4, (me_t, 2 * far + 1 - core))

    arrived(pbuf.at[0], 2)
    packed = pbuf[:, :, 64:96, :].reshape(512, 128)
    q = lax.rem(me_p, NP // 2)
    r = lax.broadcasted_iota(jnp.int32, (16, 128), 0)
    c = lax.broadcasted_iota(jnp.int32, (16, 128), 1)
    want = jnp.where(r < 8, 8 * q + r, 56 + 8 * q + r)
    rows_b = dot_nt((c == want).astype(F32).astype(BF16), packed).astype(BF16)

    arrived(cown.at[0], 3)
    none = jnp.zeros((64, 128), BF16)
    weights = []
    for part in split(cown[...].reshape(64, 128)):
        weights.append(jnp.concatenate([part, none], axis=1))
        weights.append(jnp.concatenate([none, part], axis=1))
    call[pl.ds(2 * date, 2)] = cown[...].astype(BF16)
    netted = dot(jnp.concatenate([packed, packed], axis=1), jnp.concatenate(weights, axis=0))
    net[...] = netted
    cw_a = pbuf[:, :, 0:32, :].reshape(512, 128).astype(F32)
    cw_b = pbuf[:, :, 32:64, :].reshape(512, 128).astype(F32)
    adj_a = (cw_a * jax.nn.sigmoid(netted[:, 0:128])).astype(BF16)
    adj_b = (cw_b * jax.nn.sigmoid(netted[:, 128:256])).astype(BF16)
    grad = dot(rows_b[0:8], adj_a) + dot(rows_b[8:16], adj_b)
    gsend[...] = grad
    gbuf[me_t] = grad
    over_trade(lambda peer: gsend, gbuf, 5)

    wide = net[...]
    soft = jnp.maximum(wide, 0.0) + jnp.log1p(jnp.exp(-jnp.abs(wide)))
    soft = jnp.sum(soft, axis=0, keepdims=True)
    exposure = (soft[:, 0:128] + soft[:, 128:256]) / 1024.0
    exsend[...] = jnp.broadcast_to(exposure, (8, 128))
    put(exsend, exbuf, 6, (me_t, lax.rem(me_p + NP // 2, NP)))

    arrived(call.at[pl.ds(0, 2)], 4)
    pulls = []
    for t in range(2):
        c_t = call[2 * t : 2 * t + 2].reshape(64, 128)
        adj = (psend[t, 0:64, :].astype(F32) * jax.nn.sigmoid(dot(bases[t], c_t))).astype(BF16)
        pulls.append(dot_nt(c_t, adj))
    high, low = split(pulls[1] * slope)
    carried = dot(bmap[...], high) + dot(bmap[...], low)
    partial = pack(((pulls[0] + carried) / 128.0).astype(BF16))
    qsend[...] = partial
    qbuf[me_t] = partial
    over_trade(lambda peer: qsend, qbuf, 7)

    arrived(gbuf.at[pl.ds(0, NT - 1)], 5)
    rows = jnp.zeros((16, 512), F32)
    for n in range(0, NT, 4):
        part = jnp.concatenate([gbuf[n + m] for m in range(4)], axis=1)
        high, low = split(part)
        rows = rows + dot(
            jnp.concatenate([high, low], axis=0), onehot[n : n + 4].reshape(512, 512)
        )
    rows = (rows[0:8] + rows[8:16]) * (notional / 32.0)
    folded = jnp.concatenate([rows[:, 0:256], rows[:, 256:512]], axis=0).astype(BF16)
    csend[...] = folded
    cbuf[me_p] = folded
    over_path(lambda peer: csend, cbuf, 8)

    arrived(qbuf.at[pl.ds(0, NT - 1)], 7)
    total = qbuf[0].astype(F32)
    for n in range(1, NT):
        total = total + qbuf[n].astype(F32)
    basis_out[0:32, :] = total[:, 0:64]
    basis_out[32:64, :] = pltpu.roll(total, 64, 1)[:, 0:64]

    arrived(exbuf, 6)
    row = lax.broadcasted_iota(jnp.int32, (2, 128), 0)
    exp_out[...] = jnp.where(row == date, exsend[0:2, :], exbuf[0:2, :])

    arrived(cbuf.at[pl.ds(0, NP - 1)], 8)
    for n in range(NP):
        t, k = n // 8, 8 * (n % 8)
        block = cbuf[n].astype(F32)
        coef_out[t, k : k + 8, 0:256] = block[0:8]
        coef_out[t, k : k + 8, 256:512] = block[8:16]

    sent(trecv.at[pl.ds(0, NT - 1)], 0)
    sent(pbuf.at[0, pl.ds(0, NZ - 1)], 1)
    sent(pbuf.at[0], 2)
    sent(cown.at[0], 3)
    sent(call.at[pl.ds(0, 2)], 4)
    sent(gbuf.at[pl.ds(0, NT - 1)], 5)
    sent(exbuf, 6)
    sent(qbuf.at[pl.ds(0, NT - 1)], 7)
    sent(cbuf.at[pl.ds(0, NP - 1)], 8)


def deliver(exp_in, coef_in, basis_in, exp_out, coef_out, basis_out, sems):
    copies = [
        pltpu.make_async_copy(src, dst, sems.at[n])
        for n, (src, dst) in enumerate(
            ((coef_in, coef_out), (basis_in, basis_out), (exp_in, exp_out))
        )
    ]
    for copy in copies:
        copy.start()
    for copy in copies:
        copy.wait()


def shards(
    coef, membership, trade_type, type_notional, basis_start, shocks, basis_map, credit_weight
):
    vmem = pl.BlockSpec(memory_space=pltpu.VMEM)
    hbm = pl.BlockSpec(memory_space=pltpu.HBM)
    outs = (
        jax.ShapeDtypeStruct((2, 128), F32),
        jax.ShapeDtypeStruct((2, 64, 512), F32),
        jax.ShapeDtypeStruct((64, 64), F32),
    )
    results = pl.pallas_call(
        kernel,
        out_shape=outs,
        in_specs=[hbm] * 8,
        out_specs=(vmem, vmem, vmem),
        scratch_shapes=[
            pltpu.VMEM((32, 512), BF16),
            pltpu.VMEM((1, 512), jnp.int32),
            pltpu.VMEM((1, 512), jnp.int32),
            pltpu.VMEM((1, 8), F32),
            pltpu.VMEM((64, 64), BF16),
            pltpu.VMEM((64, 64), BF16),
            pltpu.VMEM((64, 64), BF16),
            pltpu.VMEM((NT, 128, 512), BF16),
            pltpu.VMEM((NT, 32, 128), BF16),
            pltpu.VMEM((NT, 32, 128), BF16),
            pltpu.VMEM((2, 96, 128), BF16),
            pltpu.VMEM((2, NP // 2, 96, 128), BF16),
            pltpu.VMEM((2, 32, 128), F32),
            pltpu.VMEM((32, 128), BF16),
            pltpu.VMEM((4, 32, 128), BF16),
            pltpu.VMEM((512, 256), F32),
            pltpu.VMEM((8, 128), F32),
            pltpu.VMEM((NT, 8, 128), F32),
            pltpu.VMEM((8, 128), F32),
            pltpu.VMEM((8, 128), F32),
            pltpu.VMEM((32, 128), BF16),
            pltpu.VMEM((NT, 32, 128), BF16),
            pltpu.VMEM((16, 256), BF16),
            pltpu.VMEM((NP, 16, 256), BF16),
            pltpu.SemaphoreType.DMA((9,)),
            pltpu.SemaphoreType.DMA((9,)),
            pltpu.SemaphoreType.DMA((8,)),
        ],
        compiler_params=pltpu.CompilerParams(
            collective_id=0, has_side_effects=True, vmem_limit_bytes=40 * 2**20
        ),
    )(*(pltpu.with_memory_space_constraint(v, pltpu.HBM) for v in (
        coef.reshape(4, 32, 512), membership.reshape(1, 512), trade_type.reshape(1, 512),
        type_notional.reshape(1, 8), basis_start, shocks, basis_map, credit_weight,
    )))
    return pl.pallas_call(
        deliver,
        out_shape=outs,
        in_specs=[vmem] * 3,
        out_specs=(hbm,) * 3,
        scratch_shapes=[pltpu.SemaphoreType.DMA((3,))],
    )(*(pltpu.with_memory_space_constraint(v, pltpu.VMEM) for v in results))


def solution(mesh):
    placed = (
        P(None, None, "trade"),
        P("trade"),
        P("trade"),
        P(),
        P(None, "path"),
        P(None, "path"),
        P(),
        P(None, "path", None),
    )
    return jax.shard_map(
        shards,
        mesh=mesh,
        in_specs=placed,
        out_specs=(P(None, "trade"), P(None, None, "trade"), P(None, "path")),
        check_vma=False,
    )
```

```python
import functools
import math

import jax
import jax.numpy as jnp
from jax import lax
from jax.experimental import pallas as pl
from jax.experimental.pallas import tpu as pltpu
from jax.sharding import PartitionSpec as P

MESH = pl.DeviceIdType.MESH
NT = 32
NY = 8
NP = 16
F32 = jnp.float32
BF16 = jnp.bfloat16


def dot(a, b):
    return jnp.dot(a, b, preferred_element_type=F32)


def dot_nt(a, b):
    return lax.dot_general(a, b, (((1,), (1,)), ((), ())), preferred_element_type=F32)


def split(v):
    high = v.astype(BF16)
    return high, (v - high.astype(F32)).astype(BF16)


def eye(rows, cols, shift):
    r = lax.broadcasted_iota(jnp.int32, (rows, cols), 0)
    c = lax.broadcasted_iota(jnp.int32, (rows, cols), 1)
    return (r + shift == c).astype(BF16)


def hops(offset, count):
    return min(offset, count - offset)


def farthest_first(offsets, counts):
    return sorted(offsets, key=lambda o: -sum(hops(v, n) for v, n in zip(o, counts)))


NX = NT // NY
NZ = NP // 2
TRADE_PEERS = farthest_first([(a, b) for a in range(NX) for b in range(NY)], (NX, NY))[:-1]
PATH_PEERS = farthest_first([(a, b) for a in range(NZ) for b in range(2)], (NZ, 2))[:-1]


def kernel(
    coef_in, member_in, kind_in, worth_in, start_in, shocks_in, bmap_in, cw,
    exp_out, coef_out, basis_out,
    coef, member, kind, worth, start, shocks, bmap, onehot, tsend, trecv, psend, pbuf, cown, fsend, call, net, gsend, gbuf,
    exsend, exbuf, qsend, qbuf, csend, cbuf, ssem, rsem, lsem,
):
    me_t = lax.axis_index("trade")
    me_p = lax.axis_index("path")
    x, y = lax.div(me_t, NY), lax.rem(me_t, NY)
    z, core = lax.div(me_p, 2), lax.rem(me_p, 2)
    date = lax.div(me_p, NP // 2)

    xs = [lax.rem(x + n, NX) * NY for n in range(NX)]
    ys = [lax.rem(y + n, NY) for n in range(NY)]
    zs = [lax.rem(z + n, NZ) for n in range(NZ)]
    cores = [core, 1 - core]
    trade_peers = [xs[a] + ys[b] for a, b in TRADE_PEERS]
    path_peers = [2 * zs[a] + cores[b] for a, b in PATH_PEERS]

    def put(src, dst, slot, dev):
        pltpu.make_async_remote_copy(
            src_ref=src, dst_ref=dst, send_sem=ssem.at[slot], recv_sem=rsem.at[slot],
            device_id=dev, device_id_type=MESH,
        ).start()

    def over_trade(src_of, dst, slot):
        for peer in trade_peers:
            put(src_of(peer), dst.at[me_t], slot, (peer, me_p))

    def over_path(src_of, dst, slot):
        for peer in path_peers:
            put(src_of(peer), dst.at[me_p], slot, (me_t, peer))

    def arrived(ref, slot):
        pltpu.make_async_copy(ref, ref, rsem.at[slot]).wait()

    def sent(ref, slot):
        pltpu.make_async_copy(ref, ref, ssem.at[slot]).wait()

    barrier = pltpu.get_barrier_semaphore()

    for peer in trade_peers:
        pl.semaphore_signal(barrier, inc=1, device_id=(peer, me_p), device_id_type=MESH)
    sets = pl.ds(pl.multiple_of(me_t * 128, 128), 128)
    loads = [
        pltpu.make_async_copy(src, dst, lsem.at[n])
        for n, (src, dst) in enumerate((
            (start_in, start), (shocks_in, shocks), (bmap_in, bmap), (kind_in, kind),
            (worth_in, worth), (member_in, member), (coef_in.at[2 * date + core], coef),
            (cw.at[:, :, sets], psend.at[:, 0:64, :]),
        ))
    ]
    for load in loads:
        load.start()
    for peer in path_peers:
        pl.semaphore_signal(barrier, inc=1, device_id=(me_t, peer), device_id_type=MESH)

    for load in loads[3:7]:
        load.wait()

    kinds = kind[...]
    notional = jnp.zeros(kinds.shape, F32)
    for n in range(8):
        notional = jnp.where(kinds == n, worth[0:1, n : n + 1], notional)
    high, low = split(coef[...].astype(F32) * notional)
    both = jnp.concatenate([high, low], axis=0)
    members = member[...]

    def by_set(b, carry):
        ids = lax.broadcasted_iota(jnp.int32, (128, 512), 0) + b * 128
        hot = (members == ids).astype(F32).astype(BF16)
        onehot[b] = hot
        part = dot_nt(both, hot)
        tsend[b] = (part[0:32] + part[32:64]).astype(BF16)
        return carry

    lax.fori_loop(0, NT, by_set, 0, unroll=2)
    trecv[me_t] = tsend[me_t]

    pl.semaphore_wait(barrier, NT + NP - 2)
    over_trade(lambda peer: tsend.at[peer], trecv, 0)

    for load in loads[:3] + loads[7:]:
        load.wait()
    eye64 = eye(64, 64, 0)
    left, right = eye(64, 128, 0), eye(64, 128, 64)
    start_t = dot_nt(eye64, start[...]).astype(BF16)
    later_t = jnp.tanh(dot(start_t, bmap[...]) + dot_nt(eye64, shocks[...])).astype(BF16)
    slope = 1.0 - dot_nt(eye64, later_t) ** 2
    bases = (start_t, later_t)

    def pack(v):
        return (dot(v[0:32], left) + dot(v[32:64], right)).astype(BF16)

    psend[0, 64:96, :] = pack(start_t)
    psend[1, 64:96, :] = pack(later_t)
    pbuf[core, z] = psend[date]

    for n in (4, 3, 5, 2, 6, 1, 7):
        put(psend.at[lax.div(zs[n], NZ // 2)], pbuf.at[core, z], 1, (me_t, 2 * zs[n] + core))

    arrived(pbuf.at[0, pl.ds(0, NZ - 1)], 1)
    put(pbuf.at[core], pbuf.at[core], 2, (me_t, 2 * z + 1 - core))

    arrived(trecv.at[pl.ds(0, NT - 1)], 0)
    total = trecv[0].astype(F32)
    for n in range(1, NT):
        total = total + trecv[n].astype(F32)
    mine = 2 * date + core
    cown[core] = total
    fsend[...] = total.astype(BF16)
    far = zs[NZ // 2]
    put(cown.at[core], cown.at[core], 3, (me_t, 2 * z + 1 - core))
    put(fsend, call.at[mine], 4, (me_t, 2 * far + core))
    put(fsend, call.at[mine], 4, (me_t, 2 * far + 1 - core))

    arrived(pbuf.at[0], 2)
    packed = pbuf[:, :, 64:96, :].reshape(512, 128)
    q = lax.rem(me_p, NP // 2)
    r = lax.broadcasted_iota(jnp.int32, (16, 128), 0)
    c = lax.broadcasted_iota(jnp.int32, (16, 128), 1)
    want = jnp.where(r < 8, 8 * q + r, 56 + 8 * q + r)
    rows_b = dot_nt((c == want).astype(F32).astype(BF16), packed).astype(BF16)

    arrived(cown.at[0], 3)
    none = jnp.zeros((64, 128), BF16)
    weights = []
    for part in split(cown[...].reshape(64, 128)):
        weights.append(jnp.concatenate([part, none], axis=1))
        weights.append(jnp.concatenate([none, part], axis=1))
    call[pl.ds(2 * date, 2)] = cown[...].astype(BF16)
    netted = dot(jnp.concatenate([packed, packed], axis=1), jnp.concatenate(weights, axis=0))
    net[...] = netted
    cw_a = pbuf[:, :, 0:32, :].reshape(512, 128).astype(F32)
    cw_b = pbuf[:, :, 32:64, :].reshape(512, 128).astype(F32)
    adj_a = (cw_a * jax.nn.sigmoid(netted[:, 0:128])).astype(BF16)
    adj_b = (cw_b * jax.nn.sigmoid(netted[:, 128:256])).astype(BF16)
    grad = dot(rows_b[0:8], adj_a) + dot(rows_b[8:16], adj_b)
    gsend[...] = grad.astype(BF16)
    gbuf[me_t] = grad.astype(BF16)
    over_trade(lambda peer: gsend, gbuf, 5)

    wide = net[...]
    soft = jnp.maximum(wide, 0.0) + jnp.log1p(jnp.exp(-jnp.abs(wide)))
    soft = jnp.sum(soft, axis=0, keepdims=True)
    exposure = (soft[:, 0:128] + soft[:, 128:256]) / 1024.0
    exsend[...] = jnp.broadcast_to(exposure, (8, 128))
    put(exsend, exbuf, 6, (me_t, lax.rem(me_p + NP // 2, NP)))

    arrived(call.at[pl.ds(0, 2)], 4)
    pulls = []
    for t in range(2):
        c_t = call[2 * t : 2 * t + 2].reshape(64, 128)
        adj = (psend[t, 0:64, :].astype(F32) * jax.nn.sigmoid(dot(bases[t], c_t))).astype(BF16)
        pulls.append(dot_nt(c_t, adj))
    high, low = split(pulls[1] * slope)
    carried = dot(bmap[...], high) + dot(bmap[...], low)
    partial = pack(((pulls[0] + carried) / 128.0).astype(BF16))
    qsend[...] = partial
    qbuf[me_t] = partial
    over_trade(lambda peer: qsend, qbuf, 7)

    arrived(gbuf.at[pl.ds(0, NT - 1)], 5)
    rows = jnp.zeros((8, 512), F32)
    for n in range(0, NT, 4):
        part = jnp.concatenate([gbuf[n + m] for m in range(4)], axis=1)
        rows = rows + dot(part, onehot[n : n + 4].reshape(512, 512))
    folded = jnp.concatenate([rows[:, 0:256], rows[:, 256:512]], axis=0).astype(BF16)
    csend[...] = folded
    cbuf[me_p] = folded
    over_path(lambda peer: csend, cbuf, 8)

    arrived(qbuf.at[pl.ds(0, NT - 1)], 7)
    total = qbuf[0].astype(F32)
    for n in range(1, NT):
        total = total + qbuf[n].astype(F32)
    basis_out[0:32, :] = total[:, 0:64]
    basis_out[32:64, :] = pltpu.roll(total, 64, 1)[:, 0:64]

    arrived(exbuf, 6)
    row = lax.broadcasted_iota(jnp.int32, (2, 128), 0)
    exp_out[...] = jnp.where(row == date, exsend[0:2, :], exbuf[0:2, :])

    arrived(cbuf.at[pl.ds(0, NP - 1)], 8)
    scale = notional / 32.0
    for n in range(NP):
        t, k = n // 8, 8 * (n % 8)
        block = cbuf[n].astype(F32)
        coef_out[t, k : k + 8, 0:256] = block[0:8] * scale[:, 0:256]
        coef_out[t, k : k + 8, 256:512] = block[8:16] * scale[:, 256:512]

    sent(trecv.at[pl.ds(0, NT - 1)], 0)
    sent(pbuf.at[0, pl.ds(0, NZ - 1)], 1)
    sent(pbuf.at[0], 2)
    sent(cown.at[0], 3)
    sent(call.at[pl.ds(0, 2)], 4)
    sent(gbuf.at[pl.ds(0, NT - 1)], 5)
    sent(exbuf, 6)
    sent(qbuf.at[pl.ds(0, NT - 1)], 7)
    sent(cbuf.at[pl.ds(0, NP - 1)], 8)


def deliver(exp_in, coef_in, basis_in, exp_out, coef_out, basis_out, sems):
    copies = [
        pltpu.make_async_copy(src, dst, sems.at[n])
        for n, (src, dst) in enumerate(
            ((coef_in, coef_out), (basis_in, basis_out), (exp_in, exp_out))
        )
    ]
    for copy in copies:
        copy.start()
    for copy in copies:
        copy.wait()


def shards(
    coef, membership, trade_type, type_notional, basis_start, shocks, basis_map, credit_weight
):
    vmem = pl.BlockSpec(memory_space=pltpu.VMEM)
    hbm = pl.BlockSpec(memory_space=pltpu.HBM)
    outs = (
        jax.ShapeDtypeStruct((2, 128), F32),
        jax.ShapeDtypeStruct((2, 64, 512), F32),
        jax.ShapeDtypeStruct((64, 64), F32),
    )
    results = pl.pallas_call(
        kernel,
        out_shape=outs,
        in_specs=[hbm] * 8,
        out_specs=(vmem, vmem, vmem),
        scratch_shapes=[
            pltpu.VMEM((32, 512), BF16),
            pltpu.VMEM((1, 512), jnp.int32),
            pltpu.VMEM((1, 512), jnp.int32),
            pltpu.VMEM((1, 8), F32),
            pltpu.VMEM((64, 64), BF16),
            pltpu.VMEM((64, 64), BF16),
            pltpu.VMEM((64, 64), BF16),
            pltpu.VMEM((NT, 128, 512), BF16),
            pltpu.VMEM((NT, 32, 128), BF16),
            pltpu.VMEM((NT, 32, 128), BF16),
            pltpu.VMEM((2, 96, 128), BF16),
            pltpu.VMEM((2, NP // 2, 96, 128), BF16),
            pltpu.VMEM((2, 32, 128), F32),
            pltpu.VMEM((32, 128), BF16),
            pltpu.VMEM((4, 32, 128), BF16),
            pltpu.VMEM((512, 256), F32),
            pltpu.VMEM((8, 128), BF16),
            pltpu.VMEM((NT, 8, 128), BF16),
            pltpu.VMEM((8, 128), F32),
            pltpu.VMEM((8, 128), F32),
            pltpu.VMEM((32, 128), BF16),
            pltpu.VMEM((NT, 32, 128), BF16),
            pltpu.VMEM((16, 256), BF16),
            pltpu.VMEM((NP, 16, 256), BF16),
            pltpu.SemaphoreType.DMA((9,)),
            pltpu.SemaphoreType.DMA((9,)),
            pltpu.SemaphoreType.DMA((8,)),
        ],
        compiler_params=pltpu.CompilerParams(
            collective_id=0, has_side_effects=True, vmem_limit_bytes=40 * 2**20
        ),
    )(*(pltpu.with_memory_space_constraint(v, pltpu.HBM) for v in (
        coef.reshape(4, 32, 512), membership.reshape(1, 512), trade_type.reshape(1, 512),
        type_notional.reshape(1, 8), basis_start, shocks, basis_map, credit_weight,
    )))
    return pl.pallas_call(
        deliver,
        out_shape=outs,
        in_specs=[vmem] * 3,
        out_specs=(hbm,) * 3,
        scratch_shapes=[pltpu.SemaphoreType.DMA((3,))],
    )(*(pltpu.with_memory_space_constraint(v, pltpu.VMEM) for v in results))


def solution(mesh):
    placed = (
        P(None, None, "trade"),
        P("trade"),
        P("trade"),
        P(),
        P(None, "path"),
        P(None, "path"),
        P(),
        P(None, "path", None),
    )
    return jax.shard_map(
        shards,
        mesh=mesh,
        in_specs=placed,
        out_specs=(P(None, "trade"), P(None, None, "trade"), P(None, "path")),
        check_vma=False,
    )
```

```python
import functools
import math

import jax
import jax.numpy as jnp
from jax import lax
from jax.experimental import pallas as pl
from jax.experimental.pallas import tpu as pltpu
from jax.sharding import PartitionSpec as P

MESH = pl.DeviceIdType.MESH
NT = 32
NY = 8
NP = 16
F32 = jnp.float32
BF16 = jnp.bfloat16


def dot(a, b):
    return jnp.dot(a, b, preferred_element_type=F32)


def dot_nt(a, b):
    return lax.dot_general(a, b, (((1,), (1,)), ((), ())), preferred_element_type=F32)


def split(v):
    high = v.astype(BF16)
    return high, (v - high.astype(F32)).astype(BF16)


def eye(rows, cols, shift):
    r = lax.broadcasted_iota(jnp.int32, (rows, cols), 0)
    c = lax.broadcasted_iota(jnp.int32, (rows, cols), 1)
    return (r + shift == c).astype(BF16)


def hops(offset, count):
    return min(offset, count - offset)


def farthest_first(offsets, counts):
    return sorted(offsets, key=lambda o: -sum(hops(v, n) for v, n in zip(o, counts)))


NX = NT // NY
NZ = NP // 2
TRADE_PEERS = farthest_first([(a, b) for a in range(NX) for b in range(NY)], (NX, NY))[:-1]
PATH_PEERS = farthest_first([(a, b) for a in range(NZ) for b in range(2)], (NZ, 2))[:-1]


def kernel(
    coef_in, member_in, kind_in, worth_in, start_in, shocks_in, bmap_in, cw,
    exp_out, coef_out, basis_out,
    coef, member, kind, worth, start, shocks, bmap, onehot, tsend, trecv, psend, pbuf, cown, fsend, call, net, gsend, gbuf,
    exsend, exbuf, qsend, qbuf, csend, cbuf, ssem, rsem, lsem,
):
    me_t = lax.axis_index("trade")
    me_p = lax.axis_index("path")
    x, y = lax.div(me_t, NY), lax.rem(me_t, NY)
    z, core = lax.div(me_p, 2), lax.rem(me_p, 2)
    date = lax.div(me_p, NP // 2)

    xs = [lax.rem(x + n, NX) * NY for n in range(NX)]
    ys = [lax.rem(y + n, NY) for n in range(NY)]
    zs = [lax.rem(z + n, NZ) for n in range(NZ)]
    cores = [core, 1 - core]
    trade_peers = [xs[a] + ys[b] for a, b in TRADE_PEERS]
    path_peers = [2 * zs[a] + cores[b] for a, b in PATH_PEERS]

    def put(src, dst, slot, dev):
        pltpu.make_async_remote_copy(
            src_ref=src, dst_ref=dst, send_sem=ssem.at[slot], recv_sem=rsem.at[slot],
            device_id=dev, device_id_type=MESH,
        ).start()

    def over_trade(src_of, dst, slot):
        for peer in trade_peers:
            put(src_of(peer), dst.at[me_t], slot, (peer, me_p))

    def arrived(ref, slot):
        pltpu.make_async_copy(ref, ref, rsem.at[slot]).wait()

    def sent(ref, slot):
        pltpu.make_async_copy(ref, ref, ssem.at[slot]).wait()

    barrier = pltpu.get_barrier_semaphore()

    for peer in trade_peers:
        pl.semaphore_signal(barrier, inc=1, device_id=(peer, me_p), device_id_type=MESH)
    sets = pl.ds(pl.multiple_of(me_t * 128, 128), 128)
    loads = [
        pltpu.make_async_copy(src, dst, lsem.at[n])
        for n, (src, dst) in enumerate((
            (start_in, start), (shocks_in, shocks), (bmap_in, bmap), (kind_in, kind),
            (worth_in, worth), (member_in, member), (coef_in.at[2 * date + core], coef),
            (cw.at[:, :, sets], psend.at[:, 0:64, :]),
        ))
    ]
    for load in loads:
        load.start()
    for peer in path_peers:
        pl.semaphore_signal(barrier, inc=1, device_id=(me_t, peer), device_id_type=MESH)

    for load in loads[3:7]:
        load.wait()

    kinds = kind[...]
    notional = jnp.zeros(kinds.shape, F32)
    for n in range(8):
        notional = jnp.where(kinds == n, worth[0:1, n : n + 1], notional)
    high, low = split(coef[...].astype(F32) * notional)
    both = jnp.concatenate([high, low], axis=0)
    members = member[...]

    def by_set(b, carry):
        ids = lax.broadcasted_iota(jnp.int32, (128, 512), 0) + b * 128
        hot = (members == ids).astype(F32).astype(BF16)
        onehot[b] = hot
        part = dot_nt(both, hot)
        tsend[b] = (part[0:32] + part[32:64]).astype(BF16)
        return carry

    lax.fori_loop(0, NT, by_set, 0, unroll=2)
    trecv[me_t] = tsend[me_t]

    pl.semaphore_wait(barrier, NT + NP - 2)
    over_trade(lambda peer: tsend.at[peer], trecv, 0)

    for load in loads[:3] + loads[7:]:
        load.wait()
    eye64 = eye(64, 64, 0)
    left, right = eye(64, 128, 0), eye(64, 128, 64)
    start_t = dot_nt(eye64, start[...]).astype(BF16)
    later_t = jnp.tanh(dot(start_t, bmap[...]) + dot_nt(eye64, shocks[...])).astype(BF16)
    slope = 1.0 - dot_nt(eye64, later_t) ** 2
    bases = (start_t, later_t)

    def pack(v):
        return (dot(v[0:32], left) + dot(v[32:64], right)).astype(BF16)

    psend[0, 64:96, :] = pack(start_t)
    psend[1, 64:96, :] = pack(later_t)
    pbuf[core, z] = psend[date]

    for n in (4, 3, 5, 2, 6, 1, 7):
        put(psend.at[lax.div(zs[n], NZ // 2)], pbuf.at[core, z], 1, (me_t, 2 * zs[n] + core))

    arrived(pbuf.at[0, pl.ds(0, NZ - 1)], 1)
    put(pbuf.at[core], pbuf.at[core], 2, (me_t, 2 * z + 1 - core))

    arrived(trecv.at[pl.ds(0, NT - 1)], 0)
    total = trecv[0].astype(F32)
    for n in range(1, NT):
        total = total + trecv[n].astype(F32)
    mine = 2 * date + core
    cown[core] = total
    fsend[...] = total.astype(BF16)
    far = zs[NZ // 2]
    put(cown.at[core], cown.at[core], 3, (me_t, 2 * z + 1 - core))
    put(fsend, call.at[mine], 4, (me_t, 2 * far + core))
    put(fsend, call.at[mine], 4, (me_t, 2 * far + 1 - core))

    arrived(pbuf.at[0], 2)
    packed = pbuf[:, :, 64:96, :].reshape(512, 128)
    q = lax.rem(me_p, NP // 2)
    r = lax.broadcasted_iota(jnp.int32, (16, 128), 0)
    c = lax.broadcasted_iota(jnp.int32, (16, 128), 1)
    want = jnp.where(r < 8, 8 * q + r, 56 + 8 * q + r)
    rows_b = dot_nt((c == want).astype(F32).astype(BF16), packed).astype(BF16)

    arrived(cown.at[0], 3)
    none = jnp.zeros((64, 128), BF16)
    weights = []
    for part in split(cown[...].reshape(64, 128)):
        weights.append(jnp.concatenate([part, none], axis=1))
        weights.append(jnp.concatenate([none, part], axis=1))
    call[pl.ds(2 * date, 2)] = cown[...].astype(BF16)
    netted = dot(jnp.concatenate([packed, packed], axis=1), jnp.concatenate(weights, axis=0))
    net[...] = netted
    cw_a = pbuf[:, :, 0:32, :].reshape(512, 128).astype(F32)
    cw_b = pbuf[:, :, 32:64, :].reshape(512, 128).astype(F32)
    adj_a = (cw_a * jax.nn.sigmoid(netted[:, 0:128])).astype(BF16)
    adj_b = (cw_b * jax.nn.sigmoid(netted[:, 128:256])).astype(BF16)
    grad = dot(rows_b[0:8], adj_a) + dot(rows_b[8:16], adj_b)
    gsend[...] = grad.astype(BF16)
    gbuf[me_t] = grad.astype(BF16)
    over_trade(lambda peer: gsend, gbuf, 5)

    wide = net[...]
    soft = jnp.maximum(wide, 0.0) + jnp.log1p(jnp.exp(-jnp.abs(wide)))
    soft = jnp.sum(soft, axis=0, keepdims=True)
    exposure = (soft[:, 0:128] + soft[:, 128:256]) / 1024.0
    exsend[...] = jnp.broadcast_to(exposure, (8, 128))
    put(exsend, exbuf, 6, (me_t, lax.rem(me_p + NP // 2, NP)))

    arrived(call.at[pl.ds(0, 2)], 4)
    pulls = []
    for t in range(2):
        c_t = call[2 * t : 2 * t + 2].reshape(64, 128)
        adj = (psend[t, 0:64, :].astype(F32) * jax.nn.sigmoid(dot(bases[t], c_t))).astype(BF16)
        pulls.append(dot_nt(c_t, adj))
    high, low = split(pulls[1] * slope)
    carried = dot(bmap[...], high) + dot(bmap[...], low)
    partial = pack(((pulls[0] + carried) / 128.0).astype(BF16))
    qsend[...] = partial
    qbuf[me_t] = partial
    over_trade(lambda peer: qsend, qbuf, 7)

    arrived(gbuf.at[pl.ds(0, NT - 1)], 5)
    rows = jnp.zeros((8, 512), F32)
    for n in range(0, NT, 4):
        part = jnp.concatenate([gbuf[n + m] for m in range(4)], axis=1)
        rows = rows + dot(part, onehot[n : n + 4].reshape(512, 512))
    folded = jnp.concatenate([rows[:, 0:256], rows[:, 256:512]], axis=0).astype(BF16)
    csend[...] = folded
    cbuf[core, z] = folded
    for n in (4, 3, 5, 2, 6, 1, 7):
        put(csend, cbuf.at[core, z], 8, (me_t, 2 * zs[n] + core))

    arrived(cbuf.at[0, pl.ds(0, NZ - 1)], 8)
    put(cbuf.at[core], cbuf.at[core], 9, (me_t, 2 * z + 1 - core))

    arrived(qbuf.at[pl.ds(0, NT - 1)], 7)
    total = qbuf[0].astype(F32)
    for n in range(1, NT):
        total = total + qbuf[n].astype(F32)
    basis_out[0:32, :] = total[:, 0:64]
    basis_out[32:64, :] = pltpu.roll(total, 64, 1)[:, 0:64]

    arrived(exbuf, 6)
    row = lax.broadcasted_iota(jnp.int32, (2, 128), 0)
    exp_out[...] = jnp.where(row == date, exsend[0:2, :], exbuf[0:2, :])

    scale = notional / 32.0
    for side in cores:
        if side is not core:
            arrived(cbuf.at[0], 9)
        for n in range(NZ):
            k = pl.ds(pl.multiple_of(8 * (2 * (n % 4) + side), 8), 8)
            block = cbuf[side, n].astype(F32)
            coef_out[n // 4, k, 0:256] = block[0:8] * scale[:, 0:256]
            coef_out[n // 4, k, 256:512] = block[8:16] * scale[:, 256:512]

    sent(trecv.at[pl.ds(0, NT - 1)], 0)
    sent(pbuf.at[0, pl.ds(0, NZ - 1)], 1)
    sent(pbuf.at[0], 2)
    sent(cown.at[0], 3)
    sent(call.at[pl.ds(0, 2)], 4)
    sent(gbuf.at[pl.ds(0, NT - 1)], 5)
    sent(exbuf, 6)
    sent(qbuf.at[pl.ds(0, NT - 1)], 7)
    sent(cbuf.at[0, pl.ds(0, NZ - 1)], 8)
    sent(cbuf.at[0], 9)


def deliver(exp_in, coef_in, basis_in, exp_out, coef_out, basis_out, sems):
    copies = [
        pltpu.make_async_copy(src, dst, sems.at[n])
        for n, (src, dst) in enumerate(
            ((coef_in, coef_out), (basis_in, basis_out), (exp_in, exp_out))
        )
    ]
    for copy in copies:
        copy.start()
    for copy in copies:
        copy.wait()


def shards(
    coef, membership, trade_type, type_notional, basis_start, shocks, basis_map, credit_weight
):
    vmem = pl.BlockSpec(memory_space=pltpu.VMEM)
    hbm = pl.BlockSpec(memory_space=pltpu.HBM)
    outs = (
        jax.ShapeDtypeStruct((2, 128), F32),
        jax.ShapeDtypeStruct((2, 64, 512), F32),
        jax.ShapeDtypeStruct((64, 64), F32),
    )
    results = pl.pallas_call(
        kernel,
        out_shape=outs,
        in_specs=[hbm] * 8,
        out_specs=(vmem, vmem, vmem),
        scratch_shapes=[
            pltpu.VMEM((32, 512), BF16),
            pltpu.VMEM((1, 512), jnp.int32),
            pltpu.VMEM((1, 512), jnp.int32),
            pltpu.VMEM((1, 8), F32),
            pltpu.VMEM((64, 64), BF16),
            pltpu.VMEM((64, 64), BF16),
            pltpu.VMEM((64, 64), BF16),
            pltpu.VMEM((NT, 128, 512), BF16),
            pltpu.VMEM((NT, 32, 128), BF16),
            pltpu.VMEM((NT, 32, 128), BF16),
            pltpu.VMEM((2, 96, 128), BF16),
            pltpu.VMEM((2, NP // 2, 96, 128), BF16),
            pltpu.VMEM((2, 32, 128), F32),
            pltpu.VMEM((32, 128), BF16),
            pltpu.VMEM((4, 32, 128), BF16),
            pltpu.VMEM((512, 256), F32),
            pltpu.VMEM((8, 128), BF16),
            pltpu.VMEM((NT, 8, 128), BF16),
            pltpu.VMEM((8, 128), F32),
            pltpu.VMEM((8, 128), F32),
            pltpu.VMEM((32, 128), BF16),
            pltpu.VMEM((NT, 32, 128), BF16),
            pltpu.VMEM((16, 256), BF16),
            pltpu.VMEM((2, NP // 2, 16, 256), BF16),
            pltpu.SemaphoreType.DMA((10,)),
            pltpu.SemaphoreType.DMA((10,)),
            pltpu.SemaphoreType.DMA((8,)),
        ],
        compiler_params=pltpu.CompilerParams(
            collective_id=0, has_side_effects=True, vmem_limit_bytes=40 * 2**20
        ),
    )(*(pltpu.with_memory_space_constraint(v, pltpu.HBM) for v in (
        coef.reshape(4, 32, 512), membership.reshape(1, 512), trade_type.reshape(1, 512),
        type_notional.reshape(1, 8), basis_start, shocks, basis_map, credit_weight,
    )))
    return pl.pallas_call(
        deliver,
        out_shape=outs,
        in_specs=[vmem] * 3,
        out_specs=(hbm,) * 3,
        scratch_shapes=[pltpu.SemaphoreType.DMA((3,))],
    )(*(pltpu.with_memory_space_constraint(v, pltpu.VMEM) for v in results))


def solution(mesh):
    placed = (
        P(None, None, "trade"),
        P("trade"),
        P("trade"),
        P(),
        P(None, "path"),
        P(None, "path"),
        P(),
        P(None, "path", None),
    )
    return jax.shard_map(
        shards,
        mesh=mesh,
        in_specs=placed,
        out_specs=(P(None, "trade"), P(None, None, "trade"), P(None, "path")),
        check_vma=False,
    )
```
